32 devices in a mesh: row: 4 (over y, x), col: 8 (over z, core).
Axes of the slice: x: 2, y: 2, z: 4, core: 2. Of those that a mesh axis runs over, the one named last changes fastest.
Arguments:
- tokens: bfloat16 [128, 12288], P('col', 'row'), may hold values from -6 to 6
- w_in: bfloat16 [12288, 24576], P('row', 'col'), may hold values from -0.0546875 to 0.0546875
- w_out: bfloat16 [24576, 12288], P('col', 'row'), may hold values from -0.0390625 to 0.0390625
- grad_out: bfloat16 [128, 12288], P('col', 'row'), may hold values from -6 to 6
Outputs:
- block_out: bfloat16 [128, 12288], P('col', 'row')
- grad_tokens: bfloat16 [128, 12288], P('col', 'row')
- grad_w_in: bfloat16 [12288, 24576], P('row', 'col')
- grad_w_out: bfloat16 [24576, 12288], P('col', 'row')
The draws below stay inside these ranges and needn't reach their ends.
All inputs are finite; a program needn't handle non-finite values.
Results may differ from the reference program's by a relative error of at most 0.02.
Values may be sent and summed in bfloat16 or wider, within the bound.
A program may use at most 192 MiB of HBM per device.

```python
import jax
import jax.numpy as jnp
from jax import lax

D = 12288
FF = 24576
TOKENS = 128
N_ROW = 4
N_COL = 8


def block_levels(rng, extent, shards, smallest, largest):
    def one(axis_at, shards_of):
        steps = jax.random.uniform(jax.random.fold_in(jax.random.fold_in(rng, 6), axis_at), (shards_of,), jnp.float32, smallest / len(shards), largest / len(shards))
        return jnp.repeat(jnp.exp(steps), extent[axis_at] // shards_of).reshape((-1,) + (1,) * (len(extent) - axis_at - 1))

    loudness = one(*shards[0])
    for cut in shards[1:]:
        loudness = loudness * one(*cut)
    return loudness


def bell_draw(rng, shape, spread, most, split=(), kind=jnp.bfloat16):
    loudness = block_levels(rng, shape, split, -0.22, 0.18) if split else 1.0
    values = jax.random.normal(rng, shape, jnp.float32) * spread * loudness
    return jnp.minimum(jnp.maximum(values, -most), most).astype(kind)


def setup_inputs(seed: int = 0) -> dict:
    key_of = jax.random.split(jax.random.key(seed), 5)
    return {
        "tokens": bell_draw(key_of[0], (TOKENS, D), 1.0, 6.0, ((0, 8), (1, 4))),
        "w_in": bell_draw(key_of[1], (D, FF), D ** -0.5, 0.0546875, ((0, 4), (1, 8))),
        "w_out": bell_draw(key_of[2], (FF, D), FF ** -0.5, 0.0390625, ((0, 8), (1, 4))),
        "grad_out": bell_draw(key_of[3], (TOKENS, D), 1.0, 6.0, ((0, 8), (1, 4))),
    }


gelu_scale = 0.7978845608028654
gelu_cubic = 0.044715


def gelu_pair(value):
    inner = gelu_scale * (value + gelu_cubic * value * value * value)
    tangent = jnp.tanh(inner)
    result = 0.5 * value * (1.0 + tangent)
    slope = 0.5 * (1.0 + tangent) + 0.5 * value * (1.0 - tangent * tangent) * gelu_scale * (1.0 + 3.0 * gelu_cubic * value * value)
    return result, slope


def rounded(value):
    return lax.optimization_barrier(value.astype(jnp.bfloat16)).astype(jnp.float32)


def summed(left, right, count, transposed):
    width = left.shape[1] // count
    columns = right.shape[0] if transposed else right.shape[1]

    def step(total, index):
        start = (index * width).astype(jnp.int32)
        piece = lax.dynamic_slice_in_dim(left, start, width, 1)
        if transposed:
            other = lax.dynamic_slice_in_dim(right, start, width, 1)
            term = jnp.dot(piece, other.T, preferred_element_type=jnp.float32)
        else:
            other = lax.dynamic_slice_in_dim(right, start, width, 0)
            term = jnp.dot(piece, other, preferred_element_type=jnp.float32)
        return total + rounded(term), None

    init = jnp.zeros((left.shape[0], columns), jnp.float32)
    total, _ = lax.scan(step, init, jnp.arange(count, dtype=jnp.int32))
    return total


def reference(tokens, w_in, w_out, grad_out):
    pre = summed(tokens, w_in, N_ROW, False)
    grad_hidden = summed(grad_out, w_out, N_ROW, True)
    result, slope = gelu_pair(pre)
    hidden = result.astype(jnp.bfloat16)
    grad_pre = (grad_hidden * slope).astype(jnp.bfloat16)
    block_out = summed(hidden, w_out, N_COL, False).astype(jnp.bfloat16)
    grad_tokens = summed(grad_pre, w_in, N_COL, True).astype(jnp.bfloat16)
    grad_w_in = jnp.dot(tokens.T, grad_pre, preferred_element_type=jnp.float32).astype(jnp.bfloat16)
    grad_w_out = jnp.dot(hidden.T, grad_out, preferred_element_type=jnp.float32).astype(jnp.bfloat16)
    return (block_out, grad_tokens, grad_w_in, grad_w_out)
```

```python
import functools

import jax
import jax.numpy as jnp
from jax import lax
from jax.experimental import pallas as pl
from jax.experimental.pallas import tpu as pltpu
from jax.sharding import PartitionSpec as P

gelu_scale = 0.7978845608028654
gelu_cubic = 0.044715
TILE = 256
F32 = jnp.float32
BF16 = jnp.bfloat16


def gelu_pair(value):
    inner = gelu_scale * (value + gelu_cubic * value * value * value)
    tangent = jnp.tanh(inner)
    result = 0.5 * value * (1.0 + tangent)
    slope = 0.5 * (1.0 + tangent) + 0.5 * value * (1.0 - tangent * tangent) * gelu_scale * (
        1.0 + 3.0 * gelu_cubic * value * value
    )
    return (result, slope)


def aligned(index, size):
    return pl.ds(pl.multiple_of(index * size, size), size)


def dot_nt(left, right):
    return lax.dot_general(left, right, (((1,), (1,)), ((), ())), preferred_element_type=F32)


def kernel(
    n_row, n_col, chunk, part,
    x_ref, g_ref, w_in_hbm, w_out_hbm,
    out_ref, gt_ref, xp, gp, hid, gpre,
    w_in, w_out, terms_a, terms_b, land_a, land_b, slope, total, own_a, own_b,
    pair_a, pair_b, sums_a, sums_b, last_a, last_b,
    load_sem, ag_send, ag_recv, fw_send, fw_recv, rs_send, rs_recv, hg_send, hg_recv,
    pr_send, pr_recv, zs_send, zs_recv,
):
    r, q = lax.axis_index("row"), lax.axis_index("col")
    n_chip = n_col // 2
    z, core = q // 2, q % 2
    mate = z * 2 + (1 - core)
    n_tok, width = xp.shape
    hidden_units = hid.shape[1]
    n_chunk = hidden_units // chunk
    n_part = width // part
    rows_r = n_tok // n_row
    rows_c = n_tok // n_col

    def row_at(k):
        return lax.rem(r + k, n_row)

    def z_at(k):
        return lax.rem(z + k, n_chip)

    def load(which, j):
        if which == 0:
            return pltpu.make_async_copy(
                w_in_hbm.at[:, aligned(j, chunk)], w_in.at[:, aligned(j, chunk)], load_sem.at[0, j])
        return pltpu.make_async_copy(
            w_out_hbm.at[aligned(j, chunk), :], w_out.at[aligned(j, chunk), :], load_sem.at[1, j])

    for which in range(2):
        for j in range(n_chunk):
            load(which, j).start()

    barrier = pltpu.get_barrier_semaphore()
    for k in range(1, n_row):
        pl.semaphore_signal(barrier, inc=1, device_id={"row": row_at(k)}, device_id_type=pl.DeviceIdType.MESH)
    for k in range(1, n_chip):
        pl.semaphore_signal(barrier, inc=1, device_id={"col": z_at(k) * 2 + core}, device_id_type=pl.DeviceIdType.MESH)
    pl.semaphore_signal(barrier, inc=1, device_id={"col": mate}, device_id_type=pl.DeviceIdType.MESH)
    pl.semaphore_wait(barrier, n_row - 1 + n_chip - 1 + 1)

    def remote(src, dst, send, recv, **where):
        return pltpu.make_async_remote_copy(
            src_ref=src, dst_ref=dst, send_sem=send, recv_sem=recv,
            device_id=where, device_id_type=pl.DeviceIdType.MESH)

    blocks = (x_ref, g_ref)
    panels = (xp, gp)

    def gather_out(a, k):
        mine = panels[a].at[aligned(q, rows_c)]
        return remote(blocks[a], mine, ag_send.at[a, k], ag_recv.at[a, k], col=z_at(k) * 2 + core)

    def gather_in(a, k):
        there = panels[a].at[aligned(z_at(n_chip - k) * 2 + core, rows_c)]
        return remote(there, there, ag_send.at[a, k], ag_recv.at[a, k], col=mate)

    def forward_out(a, k):
        there = panels[a].at[aligned(z_at(n_chip - k) * 2 + core, rows_c)]
        source = blocks[a] if k == 0 else there
        return remote(source, there, fw_send.at[a, k], fw_recv.at[a, k], col=mate)

    def forward_in(a, k):
        there = panels[a].at[aligned(z_at(n_chip - k) * 2 + (1 - core), rows_c)]
        return remote(there, there, fw_send.at[a, k], fw_recv.at[a, k], col=mate)

    for a in range(2):
        for k in range(1, n_chip):
            gather_out(a, k).start()
        forward_out(a, 0).start()
    for a in range(2):
        panels[a][aligned(q, rows_c), :] = blocks[a][...]

    def finish_panel(a):
        for k in range(1, n_chip):
            gather_in(a, k).wait_recv()
            forward_out(a, k).start()
        for k in range(n_chip):
            forward_in(a, k).wait_recv()

    terms = (terms_a, terms_b)
    lands = (land_a, land_b)
    fulls = (hid, gpre)

    def scatter_out(a, j, k):
        to = row_at(k)
        cols = aligned(j, chunk)
        return remote(terms[a].at[aligned(to, rows_r), cols], lands[a].at[k - 1, :, cols],
                      rs_send.at[a, j, k], rs_recv.at[a, j, k], row=to)

    def spread_out(a, j, k):
        there = fulls[a].at[aligned(r, rows_r), aligned(j, chunk)]
        return remote(there, there, hg_send.at[a, j, k], hg_recv.at[a, j, k], row=row_at(k))

    def spread_in(a, j, k):
        there = fulls[a].at[aligned(row_at(n_row - k), rows_r), aligned(j, chunk)]
        return remote(there, there, hg_send.at[a, j, k], hg_recv.at[a, j, k], row=row_at(k))

    def first(a):
        def per_chunk(j, carry):
            load(a, j).wait()

            def per_tile(t, carry):
                at = aligned(j * (chunk // TILE) + t, TILE)
                if a == 0:
                    value = jnp.dot(xp[...], w_in[:, at], preferred_element_type=F32)
                else:
                    value = dot_nt(gp[...], w_out[at, :])
                terms[a][:, at] = value.astype(BF16)
                return carry

            lax.fori_loop(0, chunk // TILE, per_tile, 0)
            for k in range(1, n_row):
                scatter_out(a, j, k).start()
            return carry

        lax.fori_loop(0, n_chunk, per_chunk, 0)

    def middle(a):
        def per_chunk(j, carry):
            cols = aligned(j, chunk)
            total_here = terms[a][aligned(r, rows_r), cols].astype(F32)
            for k in range(1, n_row):
                scatter_out(a, j, k).wait_recv()
                total_here = total_here + lands[a][k - 1, :, cols].astype(F32)
            if a == 0:
                value, gradient = gelu_pair(total_here)
                slope[:, cols] = gradient
            else:
                value = total_here * slope[:, cols]
            fulls[a][aligned(r, rows_r), cols] = value.astype(BF16)
            for k in range(1, n_row):
                spread_out(a, j, k).start()
            return carry

        lax.fori_loop(0, n_chunk, per_chunk, 0)

    owns = (own_a, own_b)
    pairs = (pair_a, pair_b)
    sums = (sums_a, sums_b)
    lasts = (last_a, last_b)
    results = (out_ref, gt_ref)

    def pair_out(a, h):
        cols = pl.ds(h * part, part)
        return remote(owns[a].at[1 - core, :, cols], pairs[a].at[:, cols],
                      pr_send.at[a, h], pr_recv.at[a, h], col=mate)

    def chip_out(a, h, k):
        cols = pl.ds(h * part, part)
        to = z_at(k)
        return remote(sums[a].at[aligned(to, rows_c), cols], lasts[a].at[k - 1, :, cols],
                      zs_send.at[a, h, k], zs_recv.at[a, h, k], col=to * 2 + core)

    def second(a):
        def term(j, t):
            cols, at = aligned(j, chunk), aligned(t, TILE)
            if a == 0:
                return jnp.dot(hid[:, cols], w_out[cols, at], preferred_element_type=F32)
            return dot_nt(gpre[:, cols], w_in[at, cols])

        def arrive(j):
            for k in range(1, n_row):
                spread_in(a, j, k).wait_recv()

        def per_chunk(j, carry):
            arrive(j)

            def per_tile(t, carry):
                at = aligned(t, TILE)
                fresh = term(j, t)

                @pl.when(j == 0)
                def _():
                    total[:, at] = fresh

                @pl.when(j > 0)
                def _():
                    total[:, at] += fresh

                return carry

            lax.fori_loop(0, width // TILE, per_tile, 0)
            return carry

        lax.fori_loop(0, n_chunk - 1, per_chunk, 0)
        arrive(n_chunk - 1)
        for h in range(n_part):
            def last_tile(t, carry):
                at = aligned(t, TILE)
                value = term(n_chunk - 1, t)
                if n_chunk > 1:
                    value = total[:, at] + value
                value = value.astype(BF16).reshape(n_chip, 2, rows_c, TILE)
                for side in range(2):
                    owns[a][side, :, at] = value[:, side].reshape(n_chip * rows_c, TILE)
                return carry

            lax.fori_loop(h * (part // TILE), (h + 1) * (part // TILE), last_tile, 0)
            pair_out(a, h).start()
        for h in range(n_part):
            cols = pl.ds(h * part, part)
            pair_out(a, h).wait_recv()
            both = owns[a][core, :, cols].astype(F32) + pairs[a][:, cols].astype(F32)
            sums[a][:, cols] = both.astype(BF16)
            for k in range(1, n_chip):
                chip_out(a, h, k).start()

    def end(a):
        for h in range(n_part):
            cols = pl.ds(h * part, part)
            value = sums[a][aligned(z, rows_c), cols].astype(F32)
            for k in range(1, n_chip):
                chip_out(a, h, k).wait_recv()
                value = value + lasts[a][k - 1, :, cols].astype(F32)
            results[a][:, cols] = value.astype(BF16)

    finish_panel(0)
    first(0)
    finish_panel(1)
    first(1)
    middle(0)
    middle(1)
    second(0)
    second(1)
    end(0)
    end(1)

    for a in range(2):
        for k in range(1, n_chip):
            gather_out(a, k).wait_send()
        for k in range(n_chip):
            forward_out(a, k).wait_send()
        for h in range(n_part):
            pair_out(a, h).wait_send()
            for k in range(1, n_chip):
                chip_out(a, h, k).wait_send()

        def sent(j, carry):
            for k in range(1, n_row):
                scatter_out(a, j, k).wait_send()
                spread_out(a, j, k).wait_send()
            return carry

        lax.fori_loop(0, n_chunk, sent, 0)


def exchange(n_row, n_col, tokens, w_in, w_out, grad_out):
    rows_c, width = tokens.shape
    n_tok = rows_c * n_col
    rows_r = n_tok // n_row
    hidden_units = w_in.shape[1]
    n_chip = n_col // 2
    chunk = 768 if hidden_units % 768 == 0 else TILE
    part = 1536 if width % 1536 == 0 else width
    n_chunk, n_part = hidden_units // chunk, width // part
    shape = jax.ShapeDtypeStruct
    vmem = pl.BlockSpec(memory_space=pltpu.VMEM)
    hbm = pl.BlockSpec(memory_space=pl.ANY)
    dma = pltpu.SemaphoreType.DMA
    twice = lambda *dims: [pltpu.VMEM(dims, BF16)] * 2
    return pl.pallas_call(
        functools.partial(kernel, n_row, n_col, chunk, part),
        out_shape=(
            shape((rows_c, width), BF16), shape((rows_c, width), BF16),
            shape((n_tok, width), BF16), shape((n_tok, width), BF16),
            shape((n_tok, hidden_units), BF16), shape((n_tok, hidden_units), BF16),
        ),
        in_specs=[vmem, vmem, hbm, hbm],
        out_specs=[vmem] * 6,
        scratch_shapes=[
            pltpu.VMEM(w_in.shape, BF16), pltpu.VMEM(w_out.shape, BF16),
            *twice(n_tok, hidden_units),
            *twice(n_row - 1, rows_r, hidden_units),
            pltpu.VMEM((rows_r, hidden_units), F32),
            pltpu.VMEM((n_tok, width), F32),
            *twice(2, n_chip * rows_c, width),
            *twice(n_chip * rows_c, width),
            *twice(n_chip * rows_c, width),
            *twice(n_chip - 1, rows_c, width),
            dma((2, n_chunk)),
            dma((2, n_chip)), dma((2, n_chip)), dma((2, n_chip)), dma((2, n_chip)),
            dma((2, n_chunk, n_row)), dma((2, n_chunk, n_row)),
            dma((2, n_chunk, n_row)), dma((2, n_chunk, n_row)),
            dma((2, n_part)), dma((2, n_part)),
            dma((2, n_part, n_chip)), dma((2, n_part, n_chip)),
        ],
        compiler_params=pltpu.CompilerParams(
            collective_id=0, has_side_effects=True, vmem_limit_bytes=60 * 1024 * 1024),
        cost_estimate=pl.CostEstimate(
            flops=8 * n_tok * width * hidden_units,
            bytes_accessed=4 * width * hidden_units,
            transcendentals=rows_r * hidden_units),
        name="exchange",
    )(tokens, grad_out, w_in, w_out)


def per_device(n_row, n_col, tokens, w_in, w_out, grad_out):
    block_out, grad_tokens, token_panel, grad_panel, hidden, grad_pre = exchange(
        n_row, n_col, tokens, w_in, w_out, grad_out)
    grad_w_in = lax.dot_general(
        token_panel, grad_pre, (((0,), (0,)), ((), ())), preferred_element_type=F32)
    grad_w_out = lax.dot_general(
        hidden, grad_panel, (((0,), (0,)), ((), ())), preferred_element_type=F32)
    return (block_out, grad_tokens, grad_w_in.astype(BF16), grad_w_out.astype(BF16))


def solution(mesh):
    placed = (P("col", "row"), P("row", "col"), P("col", "row"), P("col", "row"))
    return jax.shard_map(
        functools.partial(per_device, mesh.shape["row"], mesh.shape["col"]),
        mesh=mesh,
        in_specs=placed,
        out_specs=(P("col", "row"), P("col", "row"), P("row", "col"), P("col", "row")),
        check_vma=False,
    )
```

```python
import functools

import jax
import jax.numpy as jnp
from jax import lax
from jax.experimental import pallas as pl
from jax.experimental.pallas import tpu as pltpu
from jax.sharding import PartitionSpec as P

gelu_scale = 0.7978845608028654
gelu_cubic = 0.044715
TILE = 768
F32 = jnp.float32
BF16 = jnp.bfloat16


def gelu_pair(value):
    inner = gelu_scale * (value + gelu_cubic * value * value * value)
    tangent = jnp.tanh(inner)
    result = 0.5 * value * (1.0 + tangent)
    slope = 0.5 * (1.0 + tangent) + 0.5 * value * (1.0 - tangent * tangent) * gelu_scale * (
        1.0 + 3.0 * gelu_cubic * value * value
    )
    return (result, slope)


def aligned(index, size):
    return pl.ds(pl.multiple_of(index * size, size), size)


def dot_nt(left, right):
    return lax.dot_general(left, right, (((1,), (1,)), ((), ())), preferred_element_type=F32)


def kernel(
    n_row, n_col, chunk, part,
    x_ref, g_ref, w_in_hbm, w_out_hbm,
    out_ref, xp, gp, hid, gpre, *rest,
):
    n_chip = n_col // 2
    ready = rest[:n_chip]
    (
        w_in, w_out, terms_a, terms_b, land_a, land_b, slope, total, own_a, own_b,
        pair_a, pair_b, sums, last,
        load_sem, ag_send, ag_recv, fw_send, fw_recv, rs_send, rs_recv, hg_send, hg_recv,
        pr_send, pr_recv, zs_send, zs_recv,
    ) = rest[n_chip:]
    r, q = lax.axis_index("row"), lax.axis_index("col")
    z, core = q // 2, q % 2
    mate = z * 2 + (1 - core)
    n_tok, width = xp.shape
    hidden_units = hid.shape[1]
    n_chunk = hidden_units // chunk
    n_part = width // part
    rows_r = n_tok // n_row
    rows_c = n_tok // n_col

    def row_at(k):
        return lax.rem(r + k, n_row)

    def z_at(k):
        return lax.rem(z + k, n_chip)

    def load(which, j):
        if which == 0:
            return pltpu.make_async_copy(
                w_in_hbm.at[:, aligned(j, chunk)], w_in.at[:, aligned(j, chunk)], load_sem.at[0, j])
        return pltpu.make_async_copy(
            w_out_hbm.at[aligned(j, chunk), :], w_out.at[aligned(j, chunk), :], load_sem.at[1, j])

    for j in range(n_chunk):
        load(0, j).start()

    barrier = pltpu.get_barrier_semaphore()
    for k in range(1, n_row):
        pl.semaphore_signal(barrier, inc=1, device_id={"row": row_at(k)}, device_id_type=pl.DeviceIdType.MESH)
    for k in range(1, n_chip):
        pl.semaphore_signal(barrier, inc=1, device_id={"col": z_at(k) * 2 + core}, device_id_type=pl.DeviceIdType.MESH)
    pl.semaphore_signal(barrier, inc=1, device_id={"col": mate}, device_id_type=pl.DeviceIdType.MESH)
    pl.semaphore_wait(barrier, n_row - 1 + n_chip - 1 + 1)

    def remote(src, dst, send, recv, **where):
        return pltpu.make_async_remote_copy(
            src_ref=src, dst_ref=dst, send_sem=send, recv_sem=recv,
            device_id=where, device_id_type=pl.DeviceIdType.MESH)

    blocks = (x_ref, g_ref)
    panels = (xp, gp)

    def gather_out(a, k):
        mine = panels[a].at[aligned(q, rows_c)]
        return remote(blocks[a], mine, ag_send.at[a, k], ag_recv.at[a, k], col=z_at(k) * 2 + core)

    def gather_in(a, k):
        there = panels[a].at[aligned(z_at(n_chip - k) * 2 + core, rows_c)]
        return remote(there, there, ag_send.at[a, k], ag_recv.at[a, k], col=mate)

    def forward_out(a, k):
        there = panels[a].at[aligned(z_at(n_chip - k) * 2 + core, rows_c)]
        source = blocks[a] if k == 0 else there
        return remote(source, there, fw_send.at[a, k], fw_recv.at[a, k], col=mate)

    def forward_in(a, k):
        there = panels[a].at[aligned(z_at(n_chip - k) * 2 + (1 - core), rows_c)]
        return remote(there, there, fw_send.at[a, k], fw_recv.at[a, k], col=mate)

    def start_panel(a):
        for k in range(1, n_chip):
            gather_out(a, k).start()
        forward_out(a, 0).start()

    start_panel(0)
    for a in range(2):
        panels[a][aligned(q, rows_c), :] = blocks[a][...]

    def finish_panel(a):
        for k in range(1, n_chip):
            gather_in(a, k).wait_recv()
            forward_out(a, k).start()
        if a == 0:
            start_panel(1)
            for j in range(n_chunk):
                load(1, j).start()
        for k in range(n_chip):
            forward_in(a, k).wait_recv()

    terms = (terms_a, terms_b)
    lands = (land_a, land_b)
    fulls = (hid, gpre)

    def scatter_out(a, j, k):
        to = row_at(k)
        cols = aligned(j, chunk)
        return remote(terms[a].at[aligned(to, rows_r), cols], lands[a].at[k - 1, :, cols],
                      rs_send.at[a, j, k], rs_recv.at[a, j, k], row=to)

    def spread_out(a, j, k):
        there = fulls[a].at[aligned(r, rows_r), aligned(j, chunk)]
        return remote(there, there, hg_send.at[a, j, k], hg_recv.at[a, j, k], row=row_at(k))

    def spread_in(a, j, k):
        there = fulls[a].at[aligned(row_at(n_row - k), rows_r), aligned(j, chunk)]
        return remote(there, there, hg_send.at[a, j, k], hg_recv.at[a, j, k], row=row_at(k))

    def first(a):
        def per_chunk(j, carry):
            load(a, j).wait()

            def per_tile(t, carry):
                at = aligned(j * (chunk // TILE) + t, TILE)
                if a == 0:
                    value = jnp.dot(xp[...], w_in[:, at], preferred_element_type=F32)
                else:
                    value = dot_nt(gp[...], w_out[at, :])
                terms[a][:, at] = value.astype(BF16)
                return carry

            lax.fori_loop(0, chunk // TILE, per_tile, 0)
            for k in range(1, n_row):
                scatter_out(a, j, k).start()
            return carry

        lax.fori_loop(0, n_chunk, per_chunk, 0)

    def middle(a):
        def per_chunk(j, carry):
            cols = aligned(j, chunk)
            total_here = terms[a][aligned(r, rows_r), cols].astype(F32)
            for k in range(1, n_row):
                scatter_out(a, j, k).wait_recv()
                total_here = total_here + lands[a][k - 1, :, cols].astype(F32)
            if a == 0:
                value, gradient = gelu_pair(total_here)
                slope[:, cols] = gradient
            else:
                value = total_here * slope[:, cols]
            fulls[a][aligned(r, rows_r), cols] = value.astype(BF16)
            for k in range(1, n_row):
                spread_out(a, j, k).start()
            return carry

        lax.fori_loop(0, n_chunk, per_chunk, 0)

    owns = (own_a, own_b)
    pairs = (pair_a, pair_b)

    def pair_out(a, h):
        cols = pl.ds(h * part, part)
        return remote(owns[a].at[1 - core, :, cols], pairs[a].at[:, cols],
                      pr_send.at[a, h], pr_recv.at[a, h], col=mate)

    def chip_out(h, k):
        cols = pl.ds(h * part, part)
        to = z_at(k)
        return remote(sums.at[aligned(to, rows_c), cols], last.at[k - 1, :, cols],
                      zs_send.at[h, k], zs_recv.at[h, k], col=to * 2 + core)

    def second(a):
        def term(j, t):
            cols, at = aligned(j, chunk), aligned(t, TILE)
            if a == 0:
                return jnp.dot(hid[:, cols], w_out[cols, at], preferred_element_type=F32)
            return dot_nt(gpre[:, cols], w_in[at, cols])

        def arrive(j):
            for k in range(1, n_row):
                spread_in(a, j, k).wait_recv()

        def per_chunk(j, carry):
            arrive(j)

            def per_tile(t, carry):
                at = aligned(t, TILE)
                fresh = term(j, t)

                @pl.when(j == 0)
                def _():
                    total[:, at] = fresh

                @pl.when(j > 0)
                def _():
                    total[:, at] += fresh

                return carry

            lax.fori_loop(0, width // TILE, per_tile, 0)
            return carry

        lax.fori_loop(0, n_chunk - 1, per_chunk, 0)
        arrive(n_chunk - 1)
        for h in range(n_part):
            def last_tile(t, carry):
                at = aligned(t, TILE)
                value = term(n_chunk - 1, t)
                if n_chunk > 1:
                    value = total[:, at] + value
                value = value.astype(BF16).reshape(n_chip, 2, rows_c, TILE)
                for side in range(2):
                    owns[a][side, :, at] = value[:, side].reshape(n_chip * rows_c, TILE)
                return carry

            lax.fori_loop(h * (part // TILE), (h + 1) * (part // TILE), last_tile, 0)
            pair_out(a, h).start()
        for h in range(n_part):
            cols = pl.ds(h * part, part)
            pair_out(a, h).wait_recv()
            if a == 0:
                both = owns[a][core, :, cols].astype(F32) + pairs[a][:, cols].astype(F32)
                sums[:, cols] = both.astype(BF16)
                for k in range(1, n_chip):
                    chip_out(h, k).start()
            else:
                for k in range(n_chip):
                    rows = aligned(z_at(k), rows_c)
                    both = owns[a][core, rows, cols].astype(F32) + pairs[a][rows, cols].astype(F32)
                    ready[k][:, cols] = both.astype(BF16)

    def end():
        for h in range(n_part):
            cols = pl.ds(h * part, part)
            value = sums[aligned(z, rows_c), cols].astype(F32)
            for k in range(1, n_chip):
                chip_out(h, k).wait_recv()
                value = value + last[k - 1, :, cols].astype(F32)
            out_ref[:, cols] = value.astype(BF16)

    finish_panel(0)
    first(0)
    finish_panel(1)
    first(1)
    middle(0)
    middle(1)
    second(0)
    second(1)
    end()

    for a in range(2):
        for k in range(1, n_chip):
            gather_out(a, k).wait_send()
        for k in range(n_chip):
            forward_out(a, k).wait_send()
        for h in range(n_part):
            pair_out(a, h).wait_send()

        def sent(j, carry):
            for k in range(1, n_row):
                scatter_out(a, j, k).wait_send()
                spread_out(a, j, k).wait_send()
            return carry

        lax.fori_loop(0, n_chunk, sent, 0)
    for h in range(n_part):
        for k in range(1, n_chip):
            chip_out(h, k).wait_send()


def exchange(n_row, n_col, tokens, w_in, w_out, grad_out):
    rows_c, width = tokens.shape
    n_tok = rows_c * n_col
    rows_r = n_tok // n_row
    hidden_units = w_in.shape[1]
    n_chip = n_col // 2
    chunk = 768 if hidden_units % 768 == 0 else TILE
    part = 1536 if width % 1536 == 0 else width
    n_chunk, n_part = hidden_units // chunk, width // part
    shape = jax.ShapeDtypeStruct
    vmem = pl.BlockSpec(memory_space=pltpu.VMEM)
    hbm = pl.BlockSpec(memory_space=pl.ANY)
    dma = pltpu.SemaphoreType.DMA
    twice = lambda *dims: [pltpu.VMEM(dims, BF16)] * 2
    return pl.pallas_call(
        functools.partial(kernel, n_row, n_col, chunk, part),
        out_shape=(
            shape((rows_c, width), BF16),
            shape((n_tok, width), BF16), shape((n_tok, width), BF16),
            shape((n_tok, hidden_units), BF16), shape((n_tok, hidden_units), BF16),
            *[shape((rows_c, width), BF16)] * n_chip,
        ),
        in_specs=[vmem, vmem, hbm, hbm],
        out_specs=[vmem] * (5 + n_chip),
        scratch_shapes=[
            pltpu.VMEM(w_in.shape, BF16), pltpu.VMEM(w_out.shape, BF16),
            *twice(n_tok, hidden_units),
            *twice(n_row - 1, rows_r, hidden_units),
            pltpu.VMEM((rows_r, hidden_units), F32),
            pltpu.VMEM((n_tok, width), F32),
            *twice(2, n_chip * rows_c, width),
            *twice(n_chip * rows_c, width),
            pltpu.VMEM((n_chip * rows_c, width), BF16),
            pltpu.VMEM((n_chip - 1, rows_c, width), BF16),
            dma((2, n_chunk)),
            dma((2, n_chip)), dma((2, n_chip)), dma((2, n_chip)), dma((2, n_chip)),
            dma((2, n_chunk, n_row)), dma((2, n_chunk, n_row)),
            dma((2, n_chunk, n_row)), dma((2, n_chunk, n_row)),
            dma((2, n_part)), dma((2, n_part)),
            dma((n_part, n_chip)), dma((n_part, n_chip)),
        ],
        compiler_params=pltpu.CompilerParams(
            collective_id=0, has_side_effects=True, vmem_limit_bytes=60 * 1024 * 1024),
        cost_estimate=pl.CostEstimate(
            flops=8 * n_tok * width * hidden_units,
            bytes_accessed=4 * width * hidden_units,
            transcendentals=rows_r * hidden_units),
        name="exchange",
    )(tokens, grad_out, w_in, w_out)


ROWS = 384
COLS = 512


def outer_kernel(xp, gpre, hid, gp, in_ref, out_ref):
    for left, right, result in ((xp, gpre, in_ref), (hid, gp, out_ref)):
        turned = left[...].T
        for at in range(0, right.shape[1], COLS):
            cols = pl.ds(at, min(COLS, right.shape[1] - at))
            result[:, cols] = jnp.dot(
                turned, right[:, cols], preferred_element_type=F32).astype(BF16)


def outer(xp, gpre, hid, gp):
    n_tok, width = xp.shape
    side = hid.shape[1]
    rows = ROWS * side // width
    left = lambda size: pl.BlockSpec((n_tok, size), lambda i: (0, i))
    right = lambda size: pl.BlockSpec((n_tok, size), lambda i: (0, 0))
    return pl.pallas_call(
        outer_kernel,
        grid=(width // ROWS,),
        out_shape=(jax.ShapeDtypeStruct((width, side), BF16), jax.ShapeDtypeStruct((side, width), BF16)),
        in_specs=[left(ROWS), right(side), left(rows), right(width)],
        out_specs=(pl.BlockSpec((ROWS, side), lambda i: (i, 0)), pl.BlockSpec((rows, width), lambda i: (i, 0))),
        compiler_params=pltpu.CompilerParams(vmem_limit_bytes=61 * 1024 * 1024),
        cost_estimate=pl.CostEstimate(
            flops=4 * n_tok * width * side, bytes_accessed=4 * width * side, transcendentals=0),
        name="outer",
    )(xp, gpre, hid, gp)


def per_device(n_row, n_col, tokens, w_in, w_out, grad_out):
    block_out, token_panel, grad_panel, hidden, grad_pre, *ready = exchange(
        n_row, n_col, tokens, w_in, w_out, grad_out)
    n_chip = n_col // 2
    arrived = [
        lax.ppermute(ready[k], "col", [
            (z * 2 + core, (z + k) % n_chip * 2 + core) for z in range(n_chip) for core in range(2)])
        for k in range(1, n_chip)
    ]
    grad_w_in, grad_w_out = outer(token_panel, grad_pre, hidden, grad_panel)
    grad_tokens = ready[0].astype(F32)
    for term in arrived:
        grad_tokens = grad_tokens + term.astype(F32)
    return (block_out, grad_tokens.astype(BF16), grad_w_in, grad_w_out)


def solution(mesh):
    placed = (P("col", "row"), P("row", "col"), P("col", "row"), P("col", "row"))
    return jax.shard_map(
        functools.partial(per_device, mesh.shape["row"], mesh.shape["col"]),
        mesh=mesh,
        in_specs=placed,
        out_specs=(P("col", "row"), P("col", "row"), P("row", "col"), P("col", "row")),
        check_vma=False,
    )
```

```python
import functools

import jax
import jax.numpy as jnp
from jax import lax
from jax.experimental import pallas as pl
from jax.experimental.pallas import tpu as pltpu
from jax.sharding import PartitionSpec as P

gelu_scale = 0.7978845608028654
gelu_cubic = 0.044715
TILE = 768
F32 = jnp.float32
BF16 = jnp.bfloat16


def gelu_pair(value):
    inner = gelu_scale * (value + gelu_cubic * value * value * value)
    tangent = jnp.tanh(inner)
    result = 0.5 * value * (1.0 + tangent)
    slope = 0.5 * (1.0 + tangent) + 0.5 * value * (1.0 - tangent * tangent) * gelu_scale * (
        1.0 + 3.0 * gelu_cubic * value * value
    )
    return (result, slope)


def aligned(index, size):
    return pl.ds(pl.multiple_of(index * size, size), size)


def dot_nt(left, right):
    return lax.dot_general(left, right, (((1,), (1,)), ((), ())), preferred_element_type=F32)


def kernel(
    n_row, n_col, chunk, part,
    x_ref, g_ref, w_in_hbm, w_out_hbm,
    out_ref, xp, gp, hid, gpre, *rest,
):
    n_chip = n_col // 2
    ready = rest[:n_chip]
    (
        w_in, w_out, terms_a, terms_b, land_a, land_b, slope, total, own_a, own_b,
        pair_a, pair_b, sums, last,
        load_sem, ag_send, ag_recv, fw_send, fw_recv, rs_send, rs_recv, hg_send, hg_recv,
        pr_send, pr_recv, zs_send, zs_recv,
    ) = rest[n_chip:]
    r, q = lax.axis_index("row"), lax.axis_index("col")
    z, core = q // 2, q % 2
    mate = z * 2 + (1 - core)
    n_tok, width = xp.shape
    hidden_units = hid.shape[1]
    n_chunk = hidden_units // chunk
    n_part = width // part
    rows_r = n_tok // n_row
    rows_c = n_tok // n_col

    def row_at(k):
        return lax.rem(r + k, n_row)

    def z_at(k):
        return lax.rem(z + k, n_chip)

    def load(which, j):
        if which == 0:
            return pltpu.make_async_copy(
                w_in_hbm.at[:, aligned(j, chunk)], w_in.at[:, aligned(j, chunk)], load_sem.at[0, j])
        return pltpu.make_async_copy(
            w_out_hbm.at[aligned(j, chunk), :], w_out.at[aligned(j, chunk), :], load_sem.at[1, j])

    for j in range(n_chunk):
        load(0, j).start()

    barrier = pltpu.get_barrier_semaphore()
    for k in range(1, n_row):
        pl.semaphore_signal(barrier, inc=1, device_id={"row": row_at(k)}, device_id_type=pl.DeviceIdType.MESH)
    for k in range(1, n_chip):
        pl.semaphore_signal(barrier, inc=1, device_id={"col": z_at(k) * 2 + core}, device_id_type=pl.DeviceIdType.MESH)
    pl.semaphore_signal(barrier, inc=1, device_id={"col": mate}, device_id_type=pl.DeviceIdType.MESH)
    pl.semaphore_wait(barrier, n_row - 1 + n_chip - 1 + 1)

    def remote(src, dst, send, recv, **where):
        return pltpu.make_async_remote_copy(
            src_ref=src, dst_ref=dst, send_sem=send, recv_sem=recv,
            device_id=where, device_id_type=pl.DeviceIdType.MESH)

    blocks = (x_ref, g_ref)
    panels = (xp, gp)

    def gather_out(a, k):
        mine = panels[a].at[aligned(q, rows_c)]
        return remote(blocks[a], mine, ag_send.at[a, k], ag_recv.at[a, k], col=z_at(k) * 2 + core)

    def gather_in(a, k):
        there = panels[a].at[aligned(z_at(n_chip - k) * 2 + core, rows_c)]
        return remote(there, there, ag_send.at[a, k], ag_recv.at[a, k], col=mate)

    def forward_out(a, k):
        there = panels[a].at[aligned(z_at(n_chip - k) * 2 + core, rows_c)]
        source = blocks[a] if k == 0 else there
        return remote(source, there, fw_send.at[a, k], fw_recv.at[a, k], col=mate)

    def forward_in(a, k):
        there = panels[a].at[aligned(z_at(n_chip - k) * 2 + (1 - core), rows_c)]
        return remote(there, there, fw_send.at[a, k], fw_recv.at[a, k], col=mate)

    def start_panel(a):
        for k in range(1, n_chip):
            gather_out(a, k).start()
        forward_out(a, 0).start()

    start_panel(0)
    for a in range(2):
        panels[a][aligned(q, rows_c), :] = blocks[a][...]

    def finish_panel(a):
        for k in range(1, n_chip):
            gather_in(a, k).wait_recv()
            forward_out(a, k).start()
        if a == 0:
            start_panel(1)
            for j in range(n_chunk):
                load(1, j).start()
        for k in range(n_chip):
            forward_in(a, k).wait_recv()

    terms = (terms_a, terms_b)
    lands = (land_a, land_b)
    fulls = (hid, gpre)

    def scatter_out(a, j, k):
        to = row_at(k)
        cols = aligned(j, chunk)
        return remote(terms[a].at[aligned(to, rows_r), cols], lands[a].at[k - 1, :, cols],
                      rs_send.at[a, j, k], rs_recv.at[a, j, k], row=to)

    def spread_out(a, j, k):
        there = fulls[a].at[aligned(r, rows_r), aligned(j, chunk)]
        return remote(there, there, hg_send.at[a, j, k], hg_recv.at[a, j, k], row=row_at(k))

    def spread_in(a, j, k):
        there = fulls[a].at[aligned(row_at(n_row - k), rows_r), aligned(j, chunk)]
        return remote(there, there, hg_send.at[a, j, k], hg_recv.at[a, j, k], row=row_at(k))

    def first(a):
        def per_chunk(j, carry):
            load(a, j).wait()

            def per_tile(t, carry):
                at = aligned(j * (chunk // TILE) + t, TILE)
                if a == 0:
                    value = jnp.dot(xp[...], w_in[:, at], preferred_element_type=F32)
                else:
                    value = dot_nt(gp[...], w_out[at, :])
                terms[a][:, at] = value.astype(BF16)
                return carry

            lax.fori_loop(0, chunk // TILE, per_tile, 0)
            for k in range(1, n_row):
                scatter_out(a, j, k).start()
            if a == 1:
                middle(0, j)
            return carry

        lax.fori_loop(0, n_chunk, per_chunk, 0)

    def middle(a, j):
        cols = aligned(j, chunk)
        total_here = terms[a][aligned(r, rows_r), cols].astype(F32)
        for k in range(1, n_row):
            scatter_out(a, j, k).wait_recv()
            total_here = total_here + lands[a][k - 1, :, cols].astype(F32)
        if a == 0:
            value, gradient = gelu_pair(total_here)
            slope[:, cols] = gradient
        else:
            value = total_here * slope[:, cols]
        fulls[a][aligned(r, rows_r), cols] = value.astype(BF16)
        for k in range(1, n_row):
            spread_out(a, j, k).start()

    owns = (own_a, own_b)
    pairs = (pair_a, pair_b)

    def pair_out(a, h):
        cols = pl.ds(h * part, part)
        return remote(owns[a].at[1 - core, :, cols], pairs[a].at[:, cols],
                      pr_send.at[a, h], pr_recv.at[a, h], col=mate)

    def chip_out(h, k):
        cols = pl.ds(h * part, part)
        to = z_at(k)
        return remote(sums.at[aligned(to, rows_c), cols], last.at[k - 1, :, cols],
                      zs_send.at[h, k], zs_recv.at[h, k], col=to * 2 + core)

    def second(a):
        def term(j, t):
            cols, at = aligned(j, chunk), aligned(t, TILE)
            if a == 0:
                return jnp.dot(hid[:, cols], w_out[cols, at], preferred_element_type=F32)
            return dot_nt(gpre[:, cols], w_in[at, cols])

        def arrive(j):
            for k in range(1, n_row):
                spread_in(a, j, k).wait_recv()

        def per_chunk(j, carry):
            arrive(j)

            def per_tile(t, carry):
                at = aligned(t, TILE)
                fresh = term(j, t)

                @pl.when(j == 0)
                def _():
                    total[:, at] = fresh

                @pl.when(j > 0)
                def _():
                    total[:, at] += fresh

                return carry

            lax.fori_loop(0, width // TILE, per_tile, 0)
            return carry

        lax.fori_loop(0, n_chunk - 1, per_chunk, 0)
        arrive(n_chunk - 1)
        for h in range(n_part):
            def last_tile(t, carry):
                at = aligned(t, TILE)
                value = term(n_chunk - 1, t)
                if n_chunk > 1:
                    value = total[:, at] + value
                value = value.astype(BF16).reshape(n_chip, 2, rows_c, TILE)
                for side in range(2):
                    owns[a][side, :, at] = value[:, side].reshape(n_chip * rows_c, TILE)
                return carry

            lax.fori_loop(h * (part // TILE), (h + 1) * (part // TILE), last_tile, 0)
            pair_out(a, h).start()
        for h in range(n_part):
            cols = pl.ds(h * part, part)
            pair_out(a, h).wait_recv()
            if a == 0:
                both = owns[a][core, :, cols].astype(F32) + pairs[a][:, cols].astype(F32)
                sums[:, cols] = both.astype(BF16)
                for k in range(1, n_chip):
                    chip_out(h, k).start()
            else:
                for k in range(n_chip):
                    rows = aligned(z_at(k), rows_c)
                    both = owns[a][core, rows, cols].astype(F32) + pairs[a][rows, cols].astype(F32)
                    ready[k][:, cols] = both.astype(BF16)

    def end():
        for h in range(n_part):
            cols = pl.ds(h * part, part)
            value = sums[aligned(z, rows_c), cols].astype(F32)
            for k in range(1, n_chip):
                chip_out(h, k).wait_recv()
                value = value + last[k - 1, :, cols].astype(F32)
            out_ref[:, cols] = value.astype(BF16)

    finish_panel(0)
    first(0)
    finish_panel(1)
    first(1)

    def middle_one(j, carry):
        middle(1, j)
        return carry

    lax.fori_loop(0, n_chunk, middle_one, 0)
    second(0)
    second(1)
    end()

    for a in range(2):
        for k in range(1, n_chip):
            gather_out(a, k).wait_send()
        for k in range(n_chip):
            forward_out(a, k).wait_send()
        for h in range(n_part):
            pair_out(a, h).wait_send()

        def sent(j, carry):
            for k in range(1, n_row):
                scatter_out(a, j, k).wait_send()
                spread_out(a, j, k).wait_send()
            return carry

        lax.fori_loop(0, n_chunk, sent, 0)
    for h in range(n_part):
        for k in range(1, n_chip):
            chip_out(h, k).wait_send()


def exchange(n_row, n_col, tokens, w_in, w_out, grad_out):
    rows_c, width = tokens.shape
    n_tok = rows_c * n_col
    rows_r = n_tok // n_row
    hidden_units = w_in.shape[1]
    n_chip = n_col // 2
    chunk = 768 if hidden_units % 768 == 0 else TILE
    part = 1536 if width % 1536 == 0 else width
    n_chunk, n_part = hidden_units // chunk, width // part
    shape = jax.ShapeDtypeStruct
    vmem = pl.BlockSpec(memory_space=pltpu.VMEM)
    hbm = pl.BlockSpec(memory_space=pl.ANY)
    dma = pltpu.SemaphoreType.DMA
    twice = lambda *dims: [pltpu.VMEM(dims, BF16)] * 2
    return pl.pallas_call(
        functools.partial(kernel, n_row, n_col, chunk, part),
        out_shape=(
            shape((rows_c, width), BF16),
            shape((n_tok, width), BF16), shape((n_tok, width), BF16),
            shape((n_tok, hidden_units), BF16), shape((n_tok, hidden_units), BF16),
            *[shape((rows_c, width), BF16)] * n_chip,
        ),
        in_specs=[vmem, vmem, hbm, hbm],
        out_specs=[vmem] * (5 + n_chip),
        scratch_shapes=[
            pltpu.VMEM(w_in.shape, BF16), pltpu.VMEM(w_out.shape, BF16),
            *twice(n_tok, hidden_units),
            *twice(n_row - 1, rows_r, hidden_units),
            pltpu.VMEM((rows_r, hidden_units), F32),
            pltpu.VMEM((n_tok, width), F32),
            *twice(2, n_chip * rows_c, width),
            *twice(n_chip * rows_c, width),
            pltpu.VMEM((n_chip * rows_c, width), BF16),
            pltpu.VMEM((n_chip - 1, rows_c, width), BF16),
            dma((2, n_chunk)),
            dma((2, n_chip)), dma((2, n_chip)), dma((2, n_chip)), dma((2, n_chip)),
            dma((2, n_chunk, n_row)), dma((2, n_chunk, n_row)),
            dma((2, n_chunk, n_row)), dma((2, n_chunk, n_row)),
            dma((2, n_part)), dma((2, n_part)),
            dma((n_part, n_chip)), dma((n_part, n_chip)),
        ],
        compiler_params=pltpu.CompilerParams(
            collective_id=0, has_side_effects=True, vmem_limit_bytes=60 * 1024 * 1024),
        cost_estimate=pl.CostEstimate(
            flops=8 * n_tok * width * hidden_units,
            bytes_accessed=4 * width * hidden_units,
            transcendentals=rows_r * hidden_units),
        name="exchange",
    )(tokens, grad_out, w_in, w_out)


ROWS = 384
COLS = 512


def outer_kernel(xp, gpre, hid, gp, in_ref, out_ref):
    for left, right, result in ((xp, gpre, in_ref), (hid, gp, out_ref)):
        turned = left[...].T
        for at in range(0, right.shape[1], COLS):
            cols = pl.ds(at, min(COLS, right.shape[1] - at))
            result[:, cols] = jnp.dot(
                turned, right[:, cols], preferred_element_type=F32).astype(BF16)


def outer(xp, gpre, hid, gp):
    n_tok, width = xp.shape
    side = hid.shape[1]
    rows = ROWS * side // width
    left = lambda size: pl.BlockSpec((n_tok, size), lambda i: (0, i))
    right = lambda size: pl.BlockSpec((n_tok, size), lambda i: (0, 0))
    return pl.pallas_call(
        outer_kernel,
        grid=(width // ROWS,),
        out_shape=(jax.ShapeDtypeStruct((width, side), BF16), jax.ShapeDtypeStruct((side, width), BF16)),
        in_specs=[left(ROWS), right(side), left(rows), right(width)],
        out_specs=(pl.BlockSpec((ROWS, side), lambda i: (i, 0)), pl.BlockSpec((rows, width), lambda i: (i, 0))),
        compiler_params=pltpu.CompilerParams(vmem_limit_bytes=61 * 1024 * 1024),
        cost_estimate=pl.CostEstimate(
            flops=4 * n_tok * width * side, bytes_accessed=4 * width * side, transcendentals=0),
        name="outer",
    )(xp, gpre, hid, gp)


def per_device(n_row, n_col, tokens, w_in, w_out, grad_out):
    block_out, token_panel, grad_panel, hidden, grad_pre, *ready = exchange(
        n_row, n_col, tokens, w_in, w_out, grad_out)
    n_chip = n_col // 2
    arrived = [
        lax.ppermute(ready[k], "col", [
            (z * 2 + core, (z + k) % n_chip * 2 + core) for z in range(n_chip) for core in range(2)])
        for k in range(1, n_chip)
    ]
    grad_w_in, grad_w_out = outer(token_panel, grad_pre, hidden, grad_panel)
    grad_tokens = ready[0].astype(F32)
    for term in arrived:
        grad_tokens = grad_tokens + term.astype(F32)
    return (block_out, grad_tokens.astype(BF16), grad_w_in, grad_w_out)


def solution(mesh):
    placed = (P("col", "row"), P("row", "col"), P("col", "row"), P("col", "row"))
    return jax.shard_map(
        functools.partial(per_device, mesh.shape["row"], mesh.shape["col"]),
        mesh=mesh,
        in_specs=placed,
        out_specs=(P("col", "row"), P("col", "row"), P("row", "col"), P("col", "row")),
        check_vma=False,
    )
```
